256 devices in a mesh: outer: 16 (over x, y_lo, core), inner: 16 (over z, y_hi).
Axes of the slice: x: 4, y: 4 (y_hi: 2, y_lo: 2; y = y_hi * 2 + y_lo), z: 8, core: 2. Of those that a mesh axis runs over, the one named last changes fastest.
Arguments:
- queries: bfloat16 [98304, 1024], P(('outer', 'inner')), may hold values from -4.6 to 4.6
- keys: bfloat16 [98304, 128], P(('outer', 'inner')), may hold values from -4.6 to 4.6
- values: bfloat16 [98304, 128], P(('outer', 'inner')), may hold values from -5 to 5
- grad_out: bfloat16 [98304, 1024], P(('outer', 'inner')), may hold values from -5 to 5
- span_order: int32 [512], replicated, may hold values from 0 to 511, each once
Outputs:
- grad_queries: bfloat16 [98304, 1024], P(('outer', 'inner'))
- grad_keys: bfloat16 [98304, 128], P(('outer', 'inner'))
- grad_values: bfloat16 [98304, 128], P(('outer', 'inner'))
The draws below stay inside these ranges and needn't reach their ends.
Inputs may be any that keep to these rules, and one draw needn't show every extreme that they name: `span_order`: A permutation: every span number appears once.
All inputs are finite; a program needn't handle non-finite values.
Results may differ from the reference program's by a relative error of at most 0.011.
Values may be sent and summed in bfloat16 or wider, within the bound.
No kernel may reach another device: no remote copies, remote signals or barrier semaphores. Data moves between devices by JAX's collectives and lax.ppermute only.
A program may use at most 128 MiB of HBM per device.

```python
import math
import jax
import jax.numpy as jnp
from jax import lax

HEADS = 8
HEAD = 128
TOK_DEV = 384
STEPS = 4
SPAN = 192
TOKENS = 98304
N_OUTER = 16
N_INNER = 16


def draw_queries(key, part):
    key = jax.random.fold_in(key, 11)
    base = jnp.clip(jax.random.normal(key, (TOKENS, HEADS * HEAD), jnp.float32), -4.0, 4.0)
    return base.astype(jnp.bfloat16)


def draw_keys(key, part):
    key = jax.random.fold_in(key, 23)
    base = jnp.clip(jax.random.normal(key, (TOKENS, HEAD), jnp.float32), -4.0, 4.0)
    return base.astype(jnp.bfloat16)


def block_levels(rng, shape, cuts, low, largest):
    def one(position, blocks):
        heights = jax.random.uniform(jax.random.fold_in(jax.random.fold_in(rng, 6), position), (blocks,), jnp.float32, low / len(cuts), largest / len(cuts))
        return jnp.repeat(jnp.exp(heights), shape[position] // blocks).reshape((-1,) + (1,) * (len(shape) - position - 1))

    gain = one(*cuts[0])
    for cut in cuts[1:]:
        gain = gain * one(*cut)
    return gain


def scatter_about(key, extent, spread, bound, split=(), kind=jnp.bfloat16):
    gain = block_levels(key, extent, split, -0.22, 0.18) if split else 1.0
    entries = jax.random.normal(key, extent, jnp.float32) * spread * gain
    return jnp.minimum(jnp.maximum(entries, -bound), bound).astype(kind)


def setup_inputs(seed: int = 0) -> dict:
    key_of = jax.random.split(jax.random.key(seed), 6)
    queries = draw_queries(jax.random.fold_in(key_of[5], 71), 0)
    keys = draw_keys(jax.random.fold_in(key_of[5], 71), 0)
    values = scatter_about(key_of[2], (TOKENS, HEAD), 1.0, 5.0, ((0, 256),))
    grad_out = scatter_about(key_of[3], (TOKENS, HEADS * HEAD), 1.0, 5.0, ((0, 256),))
    span_order = jax.random.permutation(key_of[4], TOKENS // SPAN).astype(jnp.int32)
    return dict(queries=queries, keys=keys, values=values, grad_out=grad_out, span_order=span_order)


def window_attention(query_rows, key_value, grad_rows, query_pos, key_pos):
    inv_root = 1.0 / math.sqrt(HEAD)
    tok_rows = query_rows.shape[0]
    query_heads = query_rows.reshape(tok_rows, HEADS, HEAD).astype(jnp.float32)
    grad_heads = grad_rows.reshape(tok_rows, HEADS, HEAD).astype(jnp.float32)
    key_part = key_value[:, :HEAD].astype(jnp.float32)
    value_part = key_value[:, HEAD:].astype(jnp.float32)
    scores = jnp.einsum('thd,kd->htk', query_heads, key_part) * inv_root
    visible = key_pos[None, :] <= query_pos[:, None]
    scores = jnp.where(visible[None], scores, -jnp.inf)
    row_max = lax.optimization_barrier(jnp.max(scores, axis=2, keepdims=True))
    log_total = row_max + jnp.log(lax.optimization_barrier(jnp.sum(jnp.exp(scores - row_max), axis=2, keepdims=True)))
    probability = jnp.exp(scores - log_total)
    prob_round = lax.optimization_barrier(probability.astype(jnp.bfloat16)).astype(jnp.float32)
    attended = jnp.einsum('htk,kd->thd', prob_round, value_part).astype(jnp.bfloat16)
    attended_f = lax.optimization_barrier(attended).astype(jnp.float32)
    row_dot = lax.optimization_barrier(jnp.sum(grad_heads * attended_f, axis=2))
    grad_prob = jnp.einsum('thd,kd->htk', grad_heads, value_part)
    grad_score = probability * (grad_prob - jnp.transpose(row_dot)[:, :, None]) * inv_root
    score_round = lax.optimization_barrier(grad_score.astype(jnp.bfloat16)).astype(jnp.float32)
    grad_q = jnp.einsum('htk,kd->thd', score_round, key_part).reshape(tok_rows, HEADS * HEAD).astype(jnp.bfloat16)
    grad_k = jnp.einsum('htk,thd->kd', score_round, query_heads)
    grad_v = jnp.einsum('htk,thd->kd', prob_round, grad_heads)
    return (grad_q, jnp.concatenate([grad_k, grad_v], axis=1))

def window_blocks(block_id):
    group = block_id // N_INNER
    within = block_id % N_INNER
    listed = [group * N_INNER + (within - stride) % N_INNER for stride in range(STEPS)]
    listed.append((group - 1) % N_OUTER * N_INNER + within)
    return listed

def reference(queries, keys, values, grad_out, span_order):
    span_len = TOK_DEV // 2
    offsets = jnp.arange(span_len, dtype=jnp.int32)
    positions = (span_order[:, None] * span_len + offsets[None, :]).reshape(-1).astype(jnp.int32)
    key_value = jnp.concatenate([keys, values], axis=1)

    def visit(running, block_id):
        start = (block_id * TOK_DEV).astype(jnp.int32)
        query_rows = lax.dynamic_slice_in_dim(queries, start, TOK_DEV, 0)
        grad_rows = lax.dynamic_slice_in_dim(grad_out, start, TOK_DEV, 0)
        query_pos = lax.dynamic_slice_in_dim(positions, start, TOK_DEV, 0)
        starts = [(other * TOK_DEV).astype(jnp.int32) for other in window_blocks(block_id)]
        window_kv = jnp.concatenate([lax.dynamic_slice_in_dim(key_value, first, TOK_DEV, 0) for first in starts], axis=0)
        key_pos = jnp.concatenate([lax.dynamic_slice_in_dim(positions, first, TOK_DEV, 0) for first in starts], axis=0)
        grad_q, partial_value = window_attention(query_rows, window_kv, grad_rows, query_pos, key_pos)
        for number, first in enumerate(starts):
            piece = partial_value[number * TOK_DEV:(number + 1) * TOK_DEV]
            before = lax.dynamic_slice_in_dim(running, first, TOK_DEV, 0)
            running = lax.dynamic_update_slice_in_dim(running, before + piece, first, 0)
        return (running, grad_q)
    initial = jnp.zeros((TOKENS, 2 * HEAD), jnp.float32)
    summed, grad_blocks = lax.scan(visit, initial, jnp.arange(N_OUTER * N_INNER, dtype=jnp.int32))
    grad_queries = grad_blocks.reshape(TOKENS, HEADS * HEAD)
    return (grad_queries, summed[:, :HEAD].astype(jnp.bfloat16), summed[:, HEAD:].astype(jnp.bfloat16))
```

```python
import functools
import math

import jax
import jax.numpy as jnp
from jax import lax
from jax.experimental import pallas as pl
from jax.experimental.pallas import tpu as pltpu
from jax.sharding import PartitionSpec as P

HEADS = 8
HEAD = 128
STEPS = 4
BLOCKS = STEPS + 1
PAIRS = HEADS // 2
ROOT = 1.0 / math.sqrt(HEAD)
SCALE = ROOT * math.log2(math.e)
BIG = 1e30
SAFE = 60.0
TILE = 256
UNROLL = 4
F32 = jnp.float32
BF16 = jnp.bfloat16
VMEM = pl.BlockSpec(memory_space=pltpu.VMEM)
SMEM = pl.BlockSpec(memory_space=pltpu.SMEM)


def fold(value, op):
    rows, lanes = value.shape
    return op(value.reshape(rows // 8, 8, lanes), axis=0)


def heads_of(ref, pair):
    first = pl.multiple_of(pair * 2 * HEAD, HEAD)
    second = pl.multiple_of(first + HEAD, HEAD)
    return jnp.concatenate([ref[:, pl.ds(first, HEAD)], ref[:, pl.ds(second, HEAD)]], axis=0)


def turn(q_ref, go_ref, qs_ref, gs_ref, qt_ref, gt_ref, norm_ref):
    norm = jnp.zeros((8, 2 * q_ref.shape[0]), F32)
    for pair in range(PAIRS):
        qs_ref[pair] = heads_of(q_ref, pair)
        gs_ref[pair] = heads_of(go_ref, pair)
        turned = qs_ref[pair].T
        qt_ref[pair] = turned
        gt_ref[pair] = gs_ref[pair].T
        square = turned.astype(F32)
        norm = jnp.maximum(norm, jnp.sum(fold(square * square, jnp.sum), axis=0, keepdims=True))
    norm_ref[...] = norm


def again_kernel(spans_ref, own_ref, out_ref):
    out_ref[...] = own_ref[...]


def small(norm_ref, kv_refs):
    longest = jnp.zeros((kv_refs[0].shape[0], 1), F32)
    for ref in kv_refs:
        key = ref[:, :HEAD].astype(F32)
        longest = jnp.maximum(longest, jnp.sum(key * key, axis=1, keepdims=True))
    return jnp.max(longest) * jnp.max(norm_ref[...]) * (SCALE * SCALE) < SAFE * SAFE


def either(safe, make):
    @pl.when(safe)
    def _():
        make(False)

    @pl.when(jnp.logical_not(safe))
    def _():
        make(True)


def scores(exact, pair, spans_ref, numbers, qt_ref, gt_ref, kv_refs, prob, gprob, mask):
    tok = kv_refs[0].shape[0]
    span = tok // 2
    wide = 2 * tok
    found = {}
    for t in range(wide // TILE):
        cols = slice(t * TILE, (t + 1) * TILE)
        lane = lax.broadcasted_iota(jnp.int32, (1, TILE), 1) + t * TILE
        qpos = jnp.where((lane % tok) < span, spans_ref[0], spans_ref[1])
        for b, number in enumerate(numbers):
            s = jnp.dot(kv_refs[b][:, :HEAD], qt_ref[pair, :, cols], preferred_element_type=F32)
            g = jnp.dot(kv_refs[b][:, HEAD:], gt_ref[pair, :, cols], preferred_element_type=F32)
            if b == 0 and mask is not None:
                s = s + mask[:, cols]
            bias = [jnp.where(qpos >= spans_ref[2 * number + half], 0.0, BIG) for half in range(2)]
            top = jnp.zeros((1, TILE), F32)
            if exact:
                top = jnp.maximum(fold(s[:span], jnp.max) - bias[0], fold(s[span:], jnp.max) - bias[1])
                top = jnp.max(top, axis=0, keepdims=True) * SCALE
            total = jnp.zeros((8, TILE), F32)
            dots = jnp.zeros((8, TILE), F32)
            for half in range(2):
                part = slice(half * span, (half + 1) * span)
                rows = slice(b * tok + half * span, b * tok + (half + 1) * span)
                e = jnp.exp2(s[part] * SCALE - (top + bias[half]))
                total = total + fold(e, jnp.sum)
                dots = dots + fold(e * g[part], jnp.sum)
                prob[pair, rows, cols] = e.astype(BF16)
                gprob[pair, rows, cols] = g[part].astype(BF16)
            found[t, b] = (top, jnp.sum(total, axis=0, keepdims=True), jnp.sum(dots, axis=0, keepdims=True))
    return [
        [jnp.concatenate([found[t, b][n] for t in range(wide // TILE)], axis=1) for n in range(3)]
        for b in range(len(numbers))
    ]


def keep(ref, pair, rows):
    for n, row in enumerate(rows):
        ref[pair, n : n + 1, :] = row


def diagonal(mask):
    tok, wide = mask.shape
    key = lax.broadcasted_iota(jnp.int32, (tok, wide), 0)
    query = lax.broadcasted_iota(jnp.int32, (tok, wide), 1)
    query = jnp.where(query >= tok, query - tok, query)
    same = (key >= tok // 2) == (query >= tok // 2)
    mask[...] = jnp.where(same & (key > query), -BIG, 0.0)


def merged(found):
    best = functools.reduce(jnp.maximum, [top for top, _, _ in found])
    weights = [jnp.exp2(top - best) for top, _, _ in found]
    total = sum(w * x for w, (_, x, _) in zip(weights, found))
    product = sum(w * x for w, (_, _, x) in zip(weights, found))
    return best, total, product, weights


def scores_kernel(numbers, spans_ref, *refs):
    count = len(numbers)
    mask = before = None
    if numbers[0] == 0:
        q_ref, go_ref, kv_ref, qs_ref, gs_ref, qt_ref, gt_ref, norm_ref, prob, gprob, stats, mask = refs
        kv_refs = [kv_ref]
        turn(q_ref, go_ref, qs_ref, gs_ref, qt_ref, gt_ref, norm_ref)
        diagonal(mask)
    else:
        qt_ref, gt_ref, norm_ref = refs[:3]
        kv_refs, (before, prob, gprob, stats) = refs[3 : 3 + count], refs[3 + count :]

    def make(exact):
        def step(pair, carry):
            found = scores(exact, pair, spans_ref, numbers, qt_ref, gt_ref, kv_refs, prob, gprob, mask)
            if before is None:
                keep(stats, pair, found[0])
            else:
                best, total, product, weights = merged([[before[pair, n : n + 1, :] for n in range(3)]] + found)
                keep(stats, pair, [best, total, product] + weights)
            return carry

        lax.fori_loop(0, PAIRS, step, 0, unroll=1 if exact else UNROLL)

    either(small(norm_ref, kv_refs), make)


def grads(pair, q_ref, go_ref, rates, rowdot, prob, gprob, dscore, dk, dv):
    tok = q_ref.shape[1] // 2
    q, go = q_ref[pair], go_ref[pair]
    for b, rate in enumerate(rates):
        rows = slice(b * tok, (b + 1) * tok)
        p = prob[pair, rows, :].astype(F32) * rate
        ds = (p * (gprob[pair, rows, :].astype(F32) - rowdot)).astype(BF16)
        dscore[pair, rows, :] = ds
        dk[rows, :] += jnp.dot(ds, q, preferred_element_type=F32)
        dv[rows, :] += jnp.dot(p.astype(BF16), go, preferred_element_type=F32)


def finish(dk, dv, outs):
    for b, out in enumerate(outs):
        tok = out.shape[0]
        out[:, :HEAD] = (dk[b * tok : (b + 1) * tok, :] * ROOT).astype(out.dtype)
        out[:, HEAD:] = dv[b * tok : (b + 1) * tok, :].astype(out.dtype)


def last_kernel(
    spans_ref, q_ref, go_ref, qt_ref, gt_ref, norm_ref, stats, kv_ref, rates, dscore, dkv, prob, gprob
):
    def make(exact):
        def find(pair, carry):
            (found,) = scores(exact, pair, spans_ref, [BLOCKS - 1], qt_ref, gt_ref, [kv_ref], prob, gprob, None)
            _, total, product, weights = merged([[stats[pair, n : n + 1, :] for n in range(3)], found])
            inv = 1.0 / total
            keep(rates, pair, [weights[0] * inv, product * inv, weights[1] * inv])
            return carry

        lax.fori_loop(0, PAIRS, find, 0, unroll=1 if exact else UNROLL)

    either(small(norm_ref, [kv_ref]), make)
    dk = dv = 0.0
    for pair in range(PAIRS):
        rowdot, rate = rates[pair, 1:2, :], rates[pair, 2:3, :]
        p = prob[pair].astype(F32) * rate
        ds = (p * (gprob[pair].astype(F32) - rowdot)).astype(BF16)
        p = p.astype(BF16)
        dscore[pair] = ds
        dk = dk + jnp.dot(ds, q_ref[pair], preferred_element_type=F32)
        dv = dv + jnp.dot(p, go_ref[pair], preferred_element_type=F32)

    dkv[:, :HEAD] = (dk * ROOT).astype(BF16)
    dkv[:, HEAD:] = dv.astype(BF16)


def grads_kernel(chains, q_ref, go_ref, rates, *refs):
    stats, (prob, gprob, dscore), outs, (dk, dv) = refs[:2], refs[2:5], refs[5:-2], refs[-2:]
    dk[...] = jnp.zeros_like(dk)
    dv[...] = jnp.zeros_like(dv)

    def step(pair, carry):
        each = []
        for chain in chains:
            rate = rates[pair, 0:1, :]
            for which, row in chain:
                rate = rate * stats[which][pair, row : row + 1, :]
            each.append(rate)
        grads(pair, q_ref, go_ref, each, rates[pair, 1:2, :], prob, gprob, dscore, dk, dv)
        return carry

    lax.fori_loop(0, PAIRS, step, 0, unroll=UNROLL)
    finish(dk, dv, outs)


def own_kernel(q_ref, go_ref, rates, near, far, prob, gprob, ds_first, ds_two, ds_last, *refs):
    kv_refs, (dq_ref, dkv, kt, dscore, dk, dv) = refs[:BLOCKS], refs[BLOCKS:]
    tok = dkv.shape[0]
    dk[...] = jnp.zeros_like(dk)
    dv[...] = jnp.zeros_like(dv)
    for b, ref in enumerate(kv_refs):
        kt[:, b * tok : (b + 1) * tok] = ref[:, :HEAD].T

    def step(pair, carry):
        rate = near[pair, 3:4, :] * far[pair, 3:4, :] * rates[pair, 0:1, :]
        grads(pair, q_ref, go_ref, [rate], rates[pair, 1:2, :], prob, gprob, dscore, dk, dv)
        dqt, start = 0.0, 0
        for part in (dscore, ds_first, ds_two, ds_last):
            end = start + part.shape[1]
            dqt = dqt + jnp.dot(kt[:, start:end], part[pair], preferred_element_type=F32)
            start = end
        dq = (dqt * ROOT).T.astype(BF16)
        first = pl.multiple_of(pair * 2 * HEAD, HEAD)
        second = pl.multiple_of(first + HEAD, HEAD)
        dq_ref[:, pl.ds(first, HEAD)] = dq[:tok]
        dq_ref[:, pl.ds(second, HEAD)] = dq[tok:]
        return carry

    lax.fori_loop(0, PAIRS, step, 0, unroll=UNROLL)
    finish(dk, dv, [dkv])


def shape(dtype, *sizes):
    return jax.ShapeDtypeStruct(sizes, dtype)


def call(kernel, name, operands, outs, scratch, flops):
    return pl.pallas_call(
        kernel,
        name=name,
        out_shape=outs,
        in_specs=[SMEM if x.dtype == jnp.int32 else VMEM for x in operands],
        out_specs=[VMEM] * len(outs),
        scratch_shapes=scratch,
        cost_estimate=pl.CostEstimate(flops=flops, bytes_accessed=0, transcendentals=0),
        compiler_params=pltpu.CompilerParams(vmem_limit_bytes=14 * 2**20),
    )(*operands)


def work(tok, blocks, products):
    return 4 * blocks * products * tok * tok * HEADS * HEAD


def again(spans, kv):
    return call(again_kernel, "again", [spans, kv], [shape(BF16, *kv.shape)], [], 0)[0]


def own_scores(spans, queries, grad_out, kv):
    tok = kv.shape[0]
    wide = 2 * tok
    return call(
        functools.partial(scores_kernel, [0]),
        "own_scores",
        [spans, queries, grad_out, kv],
        [shape(BF16, PAIRS, wide, HEAD)] * 2
        + [shape(BF16, PAIRS, HEAD, wide)] * 2
        + [shape(F32, 8, wide)]
        + [shape(BF16, PAIRS, tok, wide)] * 2
        + [shape(F32, PAIRS, 8, wide)],
        [pltpu.VMEM((tok, wide), F32)],
        work(tok, 1, 2),
    )


def score(name, spans, qt, gt, norm, blocks, numbers, *before):
    tok = blocks[0].shape[0]
    keys, wide = len(blocks) * tok, 2 * tok
    return call(
        functools.partial(scores_kernel, numbers),
        name,
        [spans, qt, gt, norm, *blocks, *before],
        [shape(BF16, PAIRS, keys, wide), shape(BF16, PAIRS, keys, wide), shape(F32, PAIRS, 8, wide)],
        [],
        work(tok, len(blocks), 2),
    )


def last(spans, queries, grad_out, qt, gt, norm, stats, kv):
    tok = queries.shape[1] // 2
    wide = 2 * tok
    return call(
        last_kernel,
        "last_block",
        [spans, queries, grad_out, qt, gt, norm, stats, kv],
        [shape(F32, PAIRS, 8, wide), shape(BF16, PAIRS, tok, wide), shape(BF16, tok, 2 * HEAD)],
        [pltpu.VMEM((PAIRS, tok, wide), BF16)] * 2,
        work(tok, 1, 4),
    )


def block_grads(name, queries, grad_out, rates, near, far, prob, gprob, chains):
    tok = queries.shape[1] // 2
    keys, wide = prob.shape[1:]
    count = keys // tok
    return call(
        functools.partial(grads_kernel, chains),
        name,
        [queries, grad_out, rates, near, far, prob, gprob],
        [shape(BF16, PAIRS, keys, wide)] + [shape(BF16, tok, 2 * HEAD)] * count,
        [pltpu.VMEM((keys, HEAD), F32)] * 2,
        work(tok, count, 2),
    )


def own_grads(queries, grad_out, rates, near, far, prob, gprob, dscores, blocks):
    tok = queries.shape[1] // 2
    return call(
        own_kernel,
        "own_grads",
        [queries, grad_out, rates, near, far, prob, gprob, *dscores, *blocks],
        [shape(BF16, tok, HEADS * HEAD), shape(F32, tok, 2 * HEAD)],
        [
            pltpu.VMEM((HEAD, BLOCKS * tok), BF16),
            pltpu.VMEM((PAIRS, tok, 2 * tok), BF16),
            pltpu.VMEM((tok, HEAD), F32),
            pltpu.VMEM((tok, HEAD), F32),
        ],
        work(tok, BLOCKS, 2),
    )


def rotate(value, axis, by):
    size = lax.axis_size(axis)
    return lax.ppermute(value, axis, [(i, (i + by) % size) for i in range(size)])


def body(queries, keys, values, grad_out, span_order):
    inner_count = lax.axis_size("inner")
    outer_count = lax.axis_size("outer")
    outer_index = lax.axis_index("outer")
    inner_index = lax.axis_index("inner")
    left = lax.broadcasted_iota(jnp.int32, (keys.shape[0], 2 * HEAD), 1) < HEAD
    zero = jnp.zeros((), BF16)
    own = jnp.where(
        left, lax.pad(keys, zero, ((0, 0, 0), (0, HEAD, 0))), lax.pad(values, zero, ((0, 0, 0), (HEAD, 0, 0)))
    )
    first = rotate(own, "inner", 1)
    numbers = [outer_index * inner_count + (inner_index - stride) % inner_count for stride in range(STEPS)]
    numbers.insert(3, (outer_index - 1) % outer_count * inner_count + inner_index)
    spans = jnp.concatenate([lax.dynamic_slice_in_dim(span_order, 2 * n, 2, 0) for n in numbers])
    later = again(spans, own)
    second = rotate(later, "inner", 2)
    outer = rotate(later, "outer", 1)
    third = rotate(first, "inner", 2)

    queries, grad_out, *turns, e0, g0, s0 = own_scores(spans, queries, grad_out, own)
    e1, g1, near = score("first_scores", spans, *turns, [first], [1], s0)
    e2, g2, far = score("two_scores", spans, *turns, [second, outer], [2, 3], near)
    rates, ds3, p_third = last(spans, queries, grad_out, *turns, far, third)
    third_back = rotate(p_third, "inner", -2)
    stats = (rates, near, far)
    ds2, p_second, p_outer = block_grads("two_grads", queries, grad_out, *stats, e2, g2, [[(1, 4)], [(1, 5)]])
    second_back = rotate(p_second, "inner", -2)
    outer_back = rotate(p_outer, "outer", -1)
    ds1, p_first = block_grads("first_grads", queries, grad_out, *stats, e1, g1, [[(0, 4), (1, 3)]])
    chain = (p_first.astype(F32) + third_back.astype(F32)).astype(BF16)
    chain_back = rotate(chain, "inner", -1)
    blocks = [own, first, second, outer, third]
    grad_q, p_own = own_grads(queries, grad_out, *stats, e0, g0, [ds1, ds2, ds3], blocks)
    summed = p_own + chain_back.astype(F32) + second_back.astype(F32) + outer_back.astype(F32)
    return (grad_q, summed[:, :HEAD].astype(BF16), summed[:, HEAD:].astype(BF16))


def solution(mesh):
    rows = P(("outer", "inner"), None)
    return jax.shard_map(
        body,
        mesh=mesh,
        in_specs=(rows, rows, rows, rows, P()),
        out_specs=(rows, rows, rows),
        check_vma=False,
    )
```

```python
import functools
import math

import jax
import jax.numpy as jnp
from jax import lax
from jax.experimental import pallas as pl
from jax.experimental.pallas import tpu as pltpu
from jax.sharding import PartitionSpec as P

HEADS = 8
HEAD = 128
STEPS = 4
BLOCKS = STEPS + 1
PAIRS = HEADS // 2
ROOT = 1.0 / math.sqrt(HEAD)
SCALE = ROOT * math.log2(math.e)
BIG = 1e30
SAFE = 100.0
TILE = 256
UNROLL = 4
F32 = jnp.float32
BF16 = jnp.bfloat16
VMEM = pl.BlockSpec(memory_space=pltpu.VMEM)
SMEM = pl.BlockSpec(memory_space=pltpu.SMEM)


def fold(value, op):
    rows, lanes = value.shape
    return op(value.reshape(rows // 8, 8, lanes), axis=0)


def heads_of(ref, pair):
    first = pl.multiple_of(pair * 2 * HEAD, HEAD)
    second = pl.multiple_of(first + HEAD, HEAD)
    return jnp.concatenate([ref[:, pl.ds(first, HEAD)], ref[:, pl.ds(second, HEAD)]], axis=0)


def turn(q_ref, go_ref, qs_ref, gs_ref, qt_ref, gt_ref, norm_ref):
    norm = jnp.zeros((8, 2 * q_ref.shape[0]), F32)
    for pair in range(PAIRS):
        qs_ref[pair] = heads_of(q_ref, pair)
        gs_ref[pair] = heads_of(go_ref, pair)
        turned = qs_ref[pair].T
        qt_ref[pair] = turned
        gt_ref[pair] = gs_ref[pair].T
        square = turned.astype(F32)
        norm = jnp.maximum(norm, jnp.sum(fold(square * square, jnp.sum), axis=0, keepdims=True))
    norm_ref[...] = jnp.broadcast_to(jnp.max(norm, axis=1, keepdims=True), norm_ref.shape)


def again_kernel(spans_ref, own_ref, out_ref, bias_ref):
    out_ref[...] = own_ref[...]
    wide = bias_ref.shape[1]
    lane = lax.broadcasted_iota(jnp.int32, (1, wide), 1)
    lane = jnp.where(lane >= wide // 2, lane - wide // 2, lane)
    qpos = jnp.where(lane < wide // 4, spans_ref[0], spans_ref[1])
    for n in range(2 * BLOCKS):
        bias_ref[n : n + 1, :] = jnp.where(qpos >= spans_ref[n], 0.0, BIG)


def small(norm_ref, kv_refs):
    longest = 0.0
    for ref in kv_refs:
        key = ref[:, :HEAD].astype(F32)
        longest = jnp.maximum(longest, fold(key * key, jnp.max))
    longest = jnp.sum(jnp.max(longest, axis=0, keepdims=True))
    return longest * jnp.max(norm_ref[...]) * (SCALE * SCALE) < SAFE * SAFE


def either(safe, make):
    @pl.when(safe)
    def _():
        make(False)

    @pl.when(jnp.logical_not(safe))
    def _():
        make(True)


def scores(exact, pair, bias_ref, numbers, qt_ref, gt_ref, kv_refs, prob, gprob, mask):
    tok = kv_refs[0].shape[0]
    span = tok // 2
    wide = 2 * tok
    found = {}
    for t in range(wide // TILE):
        cols = slice(t * TILE, (t + 1) * TILE)
        for b, number in enumerate(numbers):
            s = jnp.dot(kv_refs[b][:, :HEAD], qt_ref[pair, :, cols], preferred_element_type=F32)
            g = jnp.dot(kv_refs[b][:, HEAD:], gt_ref[pair, :, cols], preferred_element_type=F32)
            if b == 0 and mask is not None:
                s = s + mask[:, cols]
            bias = [bias_ref[2 * number + half : 2 * number + half + 1, cols] for half in range(2)]
            top = jnp.zeros((1, TILE), F32)
            if exact:
                top = jnp.maximum(fold(s[:span], jnp.max) - bias[0], fold(s[span:], jnp.max) - bias[1])
                top = jnp.max(top, axis=0, keepdims=True) * SCALE
            total = jnp.zeros((8, TILE), F32)
            dots = jnp.zeros((8, TILE), F32)
            for half in range(2):
                part = slice(half * span, (half + 1) * span)
                rows = slice(b * tok + half * span, b * tok + (half + 1) * span)
                e = jnp.exp2(s[part] * SCALE - (top + bias[half]))
                total = total + fold(e, jnp.sum)
                dots = dots + fold(e * g[part], jnp.sum)
                prob[pair, rows, cols] = e.astype(BF16)
                gprob[pair, rows, cols] = g[part].astype(BF16)
            found[t, b] = (top, jnp.sum(total, axis=0, keepdims=True), jnp.sum(dots, axis=0, keepdims=True))
    return [
        [jnp.concatenate([found[t, b][n] for t in range(wide // TILE)], axis=1) for n in range(3)]
        for b in range(len(numbers))
    ]


def keep(ref, pair, rows):
    for n, row in enumerate(rows):
        ref[pair, n : n + 1, :] = row


def diagonal(mask):
    tok, wide = mask.shape
    key = lax.broadcasted_iota(jnp.int32, (tok, wide), 0)
    query = lax.broadcasted_iota(jnp.int32, (tok, wide), 1)
    query = jnp.where(query >= tok, query - tok, query)
    same = (key >= tok // 2) == (query >= tok // 2)
    mask[...] = jnp.where(same & (key > query), -BIG, 0.0)


def merged(found):
    best = functools.reduce(jnp.maximum, [top for top, _, _ in found])
    weights = [jnp.exp2(top - best) for top, _, _ in found]
    total = sum(w * x for w, (_, x, _) in zip(weights, found))
    product = sum(w * x for w, (_, _, x) in zip(weights, found))
    return best, total, product, weights


def scores_kernel(numbers, bias_ref, *refs):
    count = len(numbers)
    mask = before = None
    if numbers[0] == 0:
        q_ref, go_ref, kv_ref, qs_ref, gs_ref, qt_ref, gt_ref, norm_ref, prob, gprob, stats, mask = refs
        kv_refs = [kv_ref]
        turn(q_ref, go_ref, qs_ref, gs_ref, qt_ref, gt_ref, norm_ref)
        diagonal(mask)
    else:
        qt_ref, gt_ref, norm_ref = refs[:3]
        kv_refs, (before, prob, gprob, stats) = refs[3 : 3 + count], refs[3 + count :]

    def make(exact):
        def step(pair, carry):
            found = scores(exact, pair, bias_ref, numbers, qt_ref, gt_ref, kv_refs, prob, gprob, mask)
            if before is None:
                keep(stats, pair, found[0])
            else:
                best, total, product, weights = merged([[before[pair, n : n + 1, :] for n in range(3)]] + found)
                keep(stats, pair, [best, total, product] + weights)
            return carry

        lax.fori_loop(0, PAIRS, step, 0, unroll=1 if exact else UNROLL)

    either(small(norm_ref, kv_refs), make)


def grads(pair, q_ref, go_ref, rates, rowdot, prob, gprob, dscore, dk, dv):
    tok = q_ref.shape[1] // 2
    q, go = q_ref[pair], go_ref[pair]
    for b, rate in enumerate(rates):
        rows = slice(b * tok, (b + 1) * tok)
        p = prob[pair, rows, :].astype(F32) * rate
        ds = (p * (gprob[pair, rows, :].astype(F32) - rowdot)).astype(BF16)
        dscore[pair, rows, :] = ds
        dk[rows, :] += jnp.dot(ds, q, preferred_element_type=F32)
        dv[rows, :] += jnp.dot(p.astype(BF16), go, preferred_element_type=F32)


def finish(dk, dv, outs):
    for b, out in enumerate(outs):
        tok = out.shape[0]
        out[:, :HEAD] = (dk[b * tok : (b + 1) * tok, :] * ROOT).astype(out.dtype)
        out[:, HEAD:] = dv[b * tok : (b + 1) * tok, :].astype(out.dtype)


def last_kernel(
    bias_ref, q_ref, go_ref, qt_ref, gt_ref, norm_ref, stats, kv_ref, rates, dscore, dkv, prob, gprob
):
    def make(exact):
        def find(pair, carry):
            (found,) = scores(exact, pair, bias_ref, [BLOCKS - 1], qt_ref, gt_ref, [kv_ref], prob, gprob, None)
            _, total, product, weights = merged([[stats[pair, n : n + 1, :] for n in range(3)], found])
            inv = 1.0 / total
            keep(rates, pair, [weights[0] * inv, product * inv, weights[1] * inv])
            return carry

        lax.fori_loop(0, PAIRS, find, 0, unroll=1 if exact else UNROLL)

    either(small(norm_ref, [kv_ref]), make)
    dk = dv = 0.0
    for pair in range(PAIRS):
        rowdot, rate = rates[pair, 1:2, :], rates[pair, 2:3, :]
        p = prob[pair].astype(F32) * rate
        ds = (p * (gprob[pair].astype(F32) - rowdot)).astype(BF16)
        p = p.astype(BF16)
        dscore[pair] = ds
        dk = dk + jnp.dot(ds, q_ref[pair], preferred_element_type=F32)
        dv = dv + jnp.dot(p, go_ref[pair], preferred_element_type=F32)

    dkv[:, :HEAD] = (dk * ROOT).astype(BF16)
    dkv[:, HEAD:] = dv.astype(BF16)


def grads_kernel(chains, q_ref, go_ref, rates, *refs):
    stats, (prob, gprob, dscore), outs, (dk, dv) = refs[:2], refs[2:5], refs[5:-2], refs[-2:]
    dk[...] = jnp.zeros_like(dk)
    dv[...] = jnp.zeros_like(dv)

    def step(pair, carry):
        each = []
        for chain in chains:
            rate = rates[pair, 0:1, :]
            for which, row in chain:
                rate = rate * stats[which][pair, row : row + 1, :]
            each.append(rate)
        grads(pair, q_ref, go_ref, each, rates[pair, 1:2, :], prob, gprob, dscore, dk, dv)
        return carry

    lax.fori_loop(0, PAIRS, step, 0, unroll=UNROLL)
    finish(dk, dv, outs)


def own_kernel(q_ref, go_ref, rates, near, far, prob, gprob, ds_first, ds_two, ds_last, *refs):
    kv_refs, (dq_ref, dkv, kt, dscore, dk, dv) = refs[:BLOCKS], refs[BLOCKS:]
    tok = dkv.shape[0]
    dk[...] = jnp.zeros_like(dk)
    dv[...] = jnp.zeros_like(dv)
    for b, ref in enumerate(kv_refs):
        kt[:, b * tok : (b + 1) * tok] = ref[:, :HEAD].T

    def step(pair, carry):
        rate = near[pair, 3:4, :] * far[pair, 3:4, :] * rates[pair, 0:1, :]
        grads(pair, q_ref, go_ref, [rate], rates[pair, 1:2, :], prob, gprob, dscore, dk, dv)
        dqt, start = 0.0, 0
        for part in (dscore, ds_first, ds_two, ds_last):
            end = start + part.shape[1]
            dqt = dqt + jnp.dot(kt[:, start:end], part[pair], preferred_element_type=F32)
            start = end
        dq = (dqt * ROOT).T.astype(BF16)
        first = pl.multiple_of(pair * 2 * HEAD, HEAD)
        second = pl.multiple_of(first + HEAD, HEAD)
        dq_ref[:, pl.ds(first, HEAD)] = dq[:tok]
        dq_ref[:, pl.ds(second, HEAD)] = dq[tok:]
        return carry

    lax.fori_loop(0, PAIRS, step, 0, unroll=UNROLL)
    finish(dk, dv, [dkv])


def shape(dtype, *sizes):
    return jax.ShapeDtypeStruct(sizes, dtype)


def call(kernel, name, operands, outs, scratch, flops):
    return pl.pallas_call(
        kernel,
        name=name,
        out_shape=outs,
        in_specs=[SMEM if x.dtype == jnp.int32 else VMEM for x in operands],
        out_specs=[VMEM] * len(outs),
        scratch_shapes=scratch,
        cost_estimate=pl.CostEstimate(flops=flops, bytes_accessed=0, transcendentals=0),
        compiler_params=pltpu.CompilerParams(vmem_limit_bytes=14 * 2**20),
    )(*operands)


def work(tok, blocks, products):
    return 4 * blocks * products * tok * tok * HEADS * HEAD


def again(spans, kv):
    out = [shape(BF16, *kv.shape), shape(F32, 16, 2 * kv.shape[0])]
    return call(again_kernel, "again", [spans, kv], out, [], 0)


def own_scores(bias, queries, grad_out, kv):
    tok = kv.shape[0]
    wide = 2 * tok
    return call(
        functools.partial(scores_kernel, [0]),
        "own_scores",
        [bias, queries, grad_out, kv],
        [shape(BF16, PAIRS, wide, HEAD)] * 2
        + [shape(BF16, PAIRS, HEAD, wide)] * 2
        + [shape(F32, 8, HEAD)]
        + [shape(BF16, PAIRS, tok, wide)] * 2
        + [shape(F32, PAIRS, 8, wide)],
        [pltpu.VMEM((tok, wide), F32)],
        work(tok, 1, 2),
    )


def score(name, bias, qt, gt, norm, blocks, numbers, *before):
    tok = blocks[0].shape[0]
    keys, wide = len(blocks) * tok, 2 * tok
    return call(
        functools.partial(scores_kernel, numbers),
        name,
        [bias, qt, gt, norm, *blocks, *before],
        [shape(BF16, PAIRS, keys, wide), shape(BF16, PAIRS, keys, wide), shape(F32, PAIRS, 8, wide)],
        [],
        work(tok, len(blocks), 2),
    )


def last(bias, queries, grad_out, qt, gt, norm, stats, kv):
    tok = queries.shape[1] // 2
    wide = 2 * tok
    return call(
        last_kernel,
        "last_block",
        [bias, queries, grad_out, qt, gt, norm, stats, kv],
        [shape(F32, PAIRS, 8, wide), shape(BF16, PAIRS, tok, wide), shape(BF16, tok, 2 * HEAD)],
        [pltpu.VMEM((PAIRS, tok, wide), BF16)] * 2,
        work(tok, 1, 4),
    )


def block_grads(name, queries, grad_out, rates, near, far, prob, gprob, chains):
    tok = queries.shape[1] // 2
    keys, wide = prob.shape[1:]
    count = keys // tok
    return call(
        functools.partial(grads_kernel, chains),
        name,
        [queries, grad_out, rates, near, far, prob, gprob],
        [shape(BF16, PAIRS, keys, wide)] + [shape(BF16, tok, 2 * HEAD)] * count,
        [pltpu.VMEM((keys, HEAD), F32)] * 2,
        work(tok, count, 2),
    )


def own_grads(queries, grad_out, rates, near, far, prob, gprob, dscores, blocks):
    tok = queries.shape[1] // 2
    return call(
        own_kernel,
        "own_grads",
        [queries, grad_out, rates, near, far, prob, gprob, *dscores, *blocks],
        [shape(BF16, tok, HEADS * HEAD), shape(F32, tok, 2 * HEAD)],
        [
            pltpu.VMEM((HEAD, BLOCKS * tok), BF16),
            pltpu.VMEM((PAIRS, tok, 2 * tok), BF16),
            pltpu.VMEM((tok, HEAD), F32),
            pltpu.VMEM((tok, HEAD), F32),
        ],
        work(tok, BLOCKS, 2),
    )


def rotate(value, axis, by):
    size = lax.axis_size(axis)
    return lax.ppermute(value, axis, [(i, (i + by) % size) for i in range(size)])


def body(queries, keys, values, grad_out, span_order):
    inner_count = lax.axis_size("inner")
    outer_count = lax.axis_size("outer")
    outer_index = lax.axis_index("outer")
    inner_index = lax.axis_index("inner")
    left = lax.broadcasted_iota(jnp.int32, (keys.shape[0], 2 * HEAD), 1) < HEAD
    zero = jnp.zeros((), BF16)
    own = jnp.where(
        left, lax.pad(keys, zero, ((0, 0, 0), (0, HEAD, 0))), lax.pad(values, zero, ((0, 0, 0), (HEAD, 0, 0)))
    )
    first = rotate(own, "inner", 1)
    numbers = [outer_index * inner_count + (inner_index - stride) % inner_count for stride in range(STEPS)]
    numbers.insert(3, (outer_index - 1) % outer_count * inner_count + inner_index)
    spans = jnp.concatenate([lax.dynamic_slice_in_dim(span_order, 2 * n, 2, 0) for n in numbers])
    later, bias = again(spans, own)
    second = rotate(later, "inner", 2)
    outer = rotate(later, "outer", 1)
    third = rotate(first, "inner", 2)

    queries, grad_out, *turns, e0, g0, s0 = own_scores(bias, queries, grad_out, own)
    e1, g1, near = score("first_scores", bias, *turns, [first], [1], s0)
    e2, g2, far = score("two_scores", bias, *turns, [second, outer], [2, 3], near)
    rates, ds3, p_third = last(bias, queries, grad_out, *turns, far, third)
    third_back = rotate(p_third, "inner", -2)
    stats = (rates, near, far)
    ds2, p_second, p_outer = block_grads("two_grads", queries, grad_out, *stats, e2, g2, [[(1, 4)], [(1, 5)]])
    second_back = rotate(p_second, "inner", -2)
    outer_back = rotate(p_outer, "outer", -1)
    ds1, p_first = block_grads("first_grads", queries, grad_out, *stats, e1, g1, [[(0, 4), (1, 3)]])
    chain = (p_first.astype(F32) + third_back.astype(F32)).astype(BF16)
    chain_back = rotate(chain, "inner", -1)
    blocks = [own, first, second, outer, third]
    grad_q, p_own = own_grads(queries, grad_out, *stats, e0, g0, [ds1, ds2, ds3], blocks)
    summed = p_own + chain_back.astype(F32) + second_back.astype(F32) + outer_back.astype(F32)
    return (grad_q, summed[:, :HEAD].astype(BF16), summed[:, HEAD:].astype(BF16))


def solution(mesh):
    rows = P(("outer", "inner"), None)
    return jax.shard_map(
        body,
        mesh=mesh,
        in_specs=(rows, rows, rows, rows, P()),
        out_specs=(rows, rows, rows),
        check_vma=False,
    )
```

```python
import functools
import math

import jax
import jax.numpy as jnp
from jax import lax
from jax.experimental import pallas as pl
from jax.experimental.pallas import tpu as pltpu
from jax.sharding import PartitionSpec as P

HEADS = 8
HEAD = 128
STEPS = 4
BLOCKS = STEPS + 1
PAIRS = HEADS // 2
ROOT = 1.0 / math.sqrt(HEAD)
SCALE = ROOT * math.log2(math.e)
BIG = 1e30
SAFE = 100.0
TILE = 256
UNROLL = 4
F32 = jnp.float32
BF16 = jnp.bfloat16
VMEM = pl.BlockSpec(memory_space=pltpu.VMEM)
SMEM = pl.BlockSpec(memory_space=pltpu.SMEM)


def fold(value, op):
    rows, lanes = value.shape
    return op(value.reshape(rows // 8, 8, lanes), axis=0)


def heads_of(ref, pair):
    first = pl.multiple_of(pair * 2 * HEAD, HEAD)
    second = pl.multiple_of(first + HEAD, HEAD)
    return jnp.concatenate([ref[:, pl.ds(first, HEAD)], ref[:, pl.ds(second, HEAD)]], axis=0)


def turn(both_ref, qs_ref, gs_ref, qt_ref, gt_ref, norm_ref):
    norm = jnp.zeros((8, 2 * both_ref.shape[0]), F32)
    for pair in range(PAIRS):
        qs_ref[pair] = heads_of(both_ref, pair)
        gs_ref[pair] = heads_of(both_ref, PAIRS + pair)
        turned = qs_ref[pair].T
        qt_ref[pair] = turned
        gt_ref[pair] = gs_ref[pair].T
        square = turned.astype(F32)
        norm = jnp.maximum(norm, jnp.sum(fold(square * square, jnp.sum), axis=0, keepdims=True))
    norm_ref[...] = jnp.broadcast_to(jnp.max(norm, axis=1, keepdims=True), norm_ref.shape)


def again_kernel(spans_ref, own_ref, out_ref, bias_ref):
    out_ref[...] = own_ref[...]
    wide = bias_ref.shape[1]
    lane = lax.broadcasted_iota(jnp.int32, (1, wide), 1)
    lane = jnp.where(lane >= wide // 2, lane - wide // 2, lane)
    qpos = jnp.where(lane < wide // 4, spans_ref[0], spans_ref[1])
    for n in range(2 * BLOCKS):
        bias_ref[n : n + 1, :] = jnp.where(qpos >= spans_ref[n], 0.0, BIG)


def small(norm_ref, kv_refs):
    longest = 0.0
    for ref in kv_refs:
        key = ref[:, :HEAD].astype(F32)
        longest = jnp.maximum(longest, fold(key * key, jnp.max))
    longest = jnp.sum(jnp.max(longest, axis=0, keepdims=True))
    return longest * jnp.max(norm_ref[...]) * (SCALE * SCALE) < SAFE * SAFE


def either(safe, make):
    @pl.when(safe)
    def _():
        make(False)

    @pl.when(jnp.logical_not(safe))
    def _():
        make(True)


def scores(exact, pair, bias_ref, numbers, qt_ref, gt_ref, kv_refs, prob, gprob, mask):
    tok = kv_refs[0].shape[0]
    span = tok // 2
    wide = 2 * tok
    found = {}
    for t in range(wide // TILE):
        cols = slice(t * TILE, (t + 1) * TILE)
        for b, number in enumerate(numbers):
            s = jnp.dot(kv_refs[b][:, :HEAD], qt_ref[pair, :, cols], preferred_element_type=F32)
            g = jnp.dot(kv_refs[b][:, HEAD:], gt_ref[pair, :, cols], preferred_element_type=F32)
            if b == 0 and mask is not None:
                s = s + mask[:, cols]
            bias = [bias_ref[2 * number + half : 2 * number + half + 1, cols] for half in range(2)]
            top = jnp.zeros((1, TILE), F32)
            if exact:
                top = jnp.maximum(fold(s[:span], jnp.max) - bias[0], fold(s[span:], jnp.max) - bias[1])
                top = jnp.max(top, axis=0, keepdims=True) * SCALE
            total = jnp.zeros((8, TILE), F32)
            dots = jnp.zeros((8, TILE), F32)
            for half in range(2):
                part = slice(half * span, (half + 1) * span)
                rows = slice(b * tok + half * span, b * tok + (half + 1) * span)
                e = jnp.exp2(s[part] * SCALE - (top + bias[half]))
                total = total + fold(e, jnp.sum)
                dots = dots + fold(e * g[part], jnp.sum)
                prob[pair, rows, cols] = e.astype(BF16)
                gprob[pair, rows, cols] = g[part].astype(BF16)
            found[t, b] = (top, jnp.sum(total, axis=0, keepdims=True), jnp.sum(dots, axis=0, keepdims=True))
    return [
        [jnp.concatenate([found[t, b][n] for t in range(wide // TILE)], axis=1) for n in range(3)]
        for b in range(len(numbers))
    ]


def keep(ref, pair, rows):
    for n, row in enumerate(rows):
        ref[pair, n : n + 1, :] = row


def diagonal(mask):
    tok, wide = mask.shape
    key = lax.broadcasted_iota(jnp.int32, (tok, wide), 0)
    query = lax.broadcasted_iota(jnp.int32, (tok, wide), 1)
    query = jnp.where(query >= tok, query - tok, query)
    same = (key >= tok // 2) == (query >= tok // 2)
    mask[...] = jnp.where(same & (key > query), -BIG, 0.0)


def merged(found):
    best = functools.reduce(jnp.maximum, [top for top, _, _ in found])
    weights = [jnp.exp2(top - best) for top, _, _ in found]
    total = sum(w * x for w, (_, x, _) in zip(weights, found))
    product = sum(w * x for w, (_, _, x) in zip(weights, found))
    return best, total, product, weights


def scores_kernel(numbers, bias_ref, *refs):
    count = len(numbers)
    mask = before = None
    if numbers[0] == 0:
        both_ref, kv_ref, qs_ref, gs_ref, qt_ref, gt_ref, norm_ref, prob, gprob, stats, mask = refs
        kv_refs = [kv_ref]
        turn(both_ref, qs_ref, gs_ref, qt_ref, gt_ref, norm_ref)
        diagonal(mask)
    else:
        qt_ref, gt_ref, norm_ref = refs[:3]
        kv_refs, (before, prob, gprob, stats) = refs[3 : 3 + count], refs[3 + count :]

    def make(exact):
        def step(pair, carry):
            found = scores(exact, pair, bias_ref, numbers, qt_ref, gt_ref, kv_refs, prob, gprob, mask)
            if before is None:
                keep(stats, pair, found[0])
            else:
                best, total, product, weights = merged([[before[pair, n : n + 1, :] for n in range(3)]] + found)
                keep(stats, pair, [best, total, product] + weights)
            return carry

        lax.fori_loop(0, PAIRS, step, 0, unroll=1 if exact else UNROLL)

    either(small(norm_ref, kv_refs), make)


def grads(pair, q_ref, go_ref, rates, rowdot, prob, gprob, dscore, dk, dv, base=0):
    tok = q_ref.shape[1] // 2
    q, go = q_ref[pair], go_ref[pair]
    for b, rate in enumerate(rates):
        rows = slice(b * tok, (b + 1) * tok)
        given = slice((base + b) * tok, (base + b + 1) * tok)
        p = prob[pair, given, :].astype(F32) * rate
        ds = (p * (gprob[pair, given, :].astype(F32) - rowdot)).astype(BF16)
        dscore[pair, rows, :] = ds
        dk[rows, :] += jnp.dot(ds, q, preferred_element_type=F32)
        dv[rows, :] += jnp.dot(p.astype(BF16), go, preferred_element_type=F32)


def finish(dk, dv, outs):
    for b, out in enumerate(outs):
        tok = out.shape[0]
        out[:, :HEAD] = (dk[b * tok : (b + 1) * tok, :] * ROOT).astype(out.dtype)
        out[:, HEAD:] = dv[b * tok : (b + 1) * tok, :].astype(out.dtype)


def last_kernel(
    bias_ref, q_ref, go_ref, qt_ref, gt_ref, norm_ref, stats, kv_ref, rates, dscore, dkv, prob, gprob
):
    def make(exact):
        def find(pair, carry):
            (found,) = scores(exact, pair, bias_ref, [BLOCKS - 1], qt_ref, gt_ref, [kv_ref], prob, gprob, None)
            _, total, product, weights = merged([[stats[pair, n : n + 1, :] for n in range(3)], found])
            inv = 1.0 / total
            keep(rates, pair, [weights[0] * inv, product * inv, weights[1] * inv])
            return carry

        lax.fori_loop(0, PAIRS, find, 0, unroll=1 if exact else UNROLL)

    either(small(norm_ref, [kv_ref]), make)
    dk = dv = 0.0
    for pair in range(PAIRS):
        rowdot, rate = rates[pair, 1:2, :], rates[pair, 2:3, :]
        p = prob[pair].astype(F32) * rate
        ds = (p * (gprob[pair].astype(F32) - rowdot)).astype(BF16)
        p = p.astype(BF16)
        dscore[pair] = ds
        dk = dk + jnp.dot(ds, q_ref[pair], preferred_element_type=F32)
        dv = dv + jnp.dot(p, go_ref[pair], preferred_element_type=F32)

    dkv[:, :HEAD] = (dk * ROOT).astype(BF16)
    dkv[:, HEAD:] = dv.astype(BF16)


def grads_kernel(chains, base, q_ref, go_ref, rates, *refs):
    stats, (prob, gprob, dscore), outs, (dk, dv) = refs[:2], refs[2:5], refs[5:-2], refs[-2:]
    dk[...] = jnp.zeros_like(dk)
    dv[...] = jnp.zeros_like(dv)

    def step(pair, carry):
        each = []
        for chain in chains:
            rate = rates[pair, 0:1, :]
            for which, row in chain:
                rate = rate * stats[which][pair, row : row + 1, :]
            each.append(rate)
        grads(pair, q_ref, go_ref, each, rates[pair, 1:2, :], prob, gprob, dscore, dk, dv, base)
        return carry

    lax.fori_loop(0, PAIRS, step, 0, unroll=UNROLL)
    finish(dk, dv, outs)


def own_kernel(q_ref, go_ref, rates, near, far, prob, gprob, *refs):
    kv_refs, (dq_ref, dkv, kt, dscore, dk, dv) = refs[-6 - BLOCKS : -6], refs[-6:]
    others = refs[: -6 - BLOCKS]
    tok = dkv.shape[0]
    dk[...] = jnp.zeros_like(dk)
    dv[...] = jnp.zeros_like(dv)
    for b, ref in enumerate(kv_refs):
        kt[:, b * tok : (b + 1) * tok] = ref[:, :HEAD].T

    def step(pair, carry):
        rate = near[pair, 3:4, :] * far[pair, 3:4, :] * rates[pair, 0:1, :]
        grads(pair, q_ref, go_ref, [rate], rates[pair, 1:2, :], prob, gprob, dscore, dk, dv)
        dqt, start = 0.0, 0
        for part in (dscore, *others):
            end = start + part.shape[1]
            dqt = dqt + jnp.dot(kt[:, start:end], part[pair], preferred_element_type=F32)
            start = end
        dq = (dqt * ROOT).T.astype(BF16)
        first = pl.multiple_of(pair * 2 * HEAD, HEAD)
        second = pl.multiple_of(first + HEAD, HEAD)
        dq_ref[:, pl.ds(first, HEAD)] = dq[:tok]
        dq_ref[:, pl.ds(second, HEAD)] = dq[tok:]
        return carry

    lax.fori_loop(0, PAIRS, step, 0, unroll=UNROLL)
    finish(dk, dv, [dkv])


def shape(dtype, *sizes):
    return jax.ShapeDtypeStruct(sizes, dtype)


def call(kernel, name, operands, outs, scratch, flops):
    return pl.pallas_call(
        kernel,
        name=name,
        out_shape=outs,
        in_specs=[SMEM if x.dtype == jnp.int32 else VMEM for x in operands],
        out_specs=[VMEM] * len(outs),
        scratch_shapes=scratch,
        cost_estimate=pl.CostEstimate(flops=flops, bytes_accessed=0, transcendentals=0),
        compiler_params=pltpu.CompilerParams(vmem_limit_bytes=14 * 2**20),
    )(*operands)


def work(tok, blocks, products):
    return 4 * blocks * products * tok * tok * HEADS * HEAD


def again(spans, kv):
    out = [shape(BF16, *kv.shape), shape(F32, 16, 2 * kv.shape[0])]
    return call(again_kernel, "again", [spans, kv], out, [], 0)


def own_scores(bias, both, kv):
    tok = kv.shape[0]
    wide = 2 * tok
    return call(
        functools.partial(scores_kernel, [0]),
        "own_scores",
        [bias, both, kv],
        [shape(BF16, PAIRS, wide, HEAD)] * 2
        + [shape(BF16, PAIRS, HEAD, wide)] * 2
        + [shape(F32, 8, HEAD)]
        + [shape(BF16, PAIRS, tok, wide)] * 2
        + [shape(F32, PAIRS, 8, wide)],
        [pltpu.VMEM((tok, wide), F32)],
        work(tok, 1, 2),
    )


def score(name, bias, qt, gt, norm, blocks, numbers, *before):
    tok = blocks[0].shape[0]
    keys, wide = len(blocks) * tok, 2 * tok
    return call(
        functools.partial(scores_kernel, numbers),
        name,
        [bias, qt, gt, norm, *blocks, *before],
        [shape(BF16, PAIRS, keys, wide), shape(BF16, PAIRS, keys, wide), shape(F32, PAIRS, 8, wide)],
        [],
        work(tok, len(blocks), 2),
    )


def last(bias, queries, grad_out, qt, gt, norm, stats, kv):
    tok = queries.shape[1] // 2
    wide = 2 * tok
    return call(
        last_kernel,
        "last_block",
        [bias, queries, grad_out, qt, gt, norm, stats, kv],
        [shape(F32, PAIRS, 8, wide), shape(BF16, PAIRS, tok, wide), shape(BF16, tok, 2 * HEAD)],
        [pltpu.VMEM((PAIRS, tok, wide), BF16)] * 2,
        work(tok, 1, 4),
    )


def block_grads(name, queries, grad_out, rates, near, far, prob, gprob, chains, base=0):
    tok = queries.shape[1] // 2
    wide = prob.shape[2]
    count = len(chains)
    return call(
        functools.partial(grads_kernel, chains, base),
        name,
        [queries, grad_out, rates, near, far, prob, gprob],
        [shape(BF16, PAIRS, count * tok, wide)] + [shape(BF16, tok, 2 * HEAD)] * count,
        [pltpu.VMEM((count * tok, HEAD), F32)] * 2,
        work(tok, count, 2),
    )


def own_grads(queries, grad_out, rates, near, far, prob, gprob, dscores, blocks):
    tok = queries.shape[1] // 2
    return call(
        own_kernel,
        "own_grads",
        [queries, grad_out, rates, near, far, prob, gprob, *dscores, *blocks],
        [shape(BF16, tok, HEADS * HEAD), shape(F32, tok, 2 * HEAD)],
        [
            pltpu.VMEM((HEAD, BLOCKS * tok), BF16),
            pltpu.VMEM((PAIRS, tok, 2 * tok), BF16),
            pltpu.VMEM((tok, HEAD), F32),
            pltpu.VMEM((tok, HEAD), F32),
        ],
        work(tok, BLOCKS, 2),
    )


def rotate(value, axis, by):
    size = lax.axis_size(axis)
    return lax.ppermute(value, axis, [(i, (i + by) % size) for i in range(size)])


def side_by_side(one, other):
    lanes = one.shape[1]
    zero = jnp.zeros((), one.dtype)
    left = lax.broadcasted_iota(jnp.int32, (one.shape[0], 2 * lanes), 1) < lanes
    return jnp.where(
        left, lax.pad(one, zero, ((0, 0, 0), (0, lanes, 0))), lax.pad(other, zero, ((0, 0, 0), (lanes, 0, 0)))
    )


def body(queries, keys, values, grad_out, span_order):
    inner_count = lax.axis_size("inner")
    outer_count = lax.axis_size("outer")
    outer_index = lax.axis_index("outer")
    inner_index = lax.axis_index("inner")
    own = side_by_side(keys, values)
    first = rotate(own, "inner", 1)
    numbers = [outer_index * inner_count + (inner_index - stride) % inner_count for stride in range(STEPS)]
    numbers.insert(3, (outer_index - 1) % outer_count * inner_count + inner_index)
    spans = jnp.concatenate([lax.dynamic_slice_in_dim(span_order, 2 * n, 2, 0) for n in numbers])
    later, bias = again(spans, own)
    second = rotate(later, "inner", 2)
    outer = rotate(later, "outer", 1)
    third = rotate(first, "inner", 2)

    queries, grad_out, *turns, e0, g0, s0 = own_scores(bias, side_by_side(queries, grad_out), own)
    e1, g1, near = score("first_scores", bias, *turns, [first], [1], s0)
    e2, g2, far = score("two_scores", bias, *turns, [second, outer], [2, 3], near)
    rates, ds3, p_third = last(bias, queries, grad_out, *turns, far, third)
    third_back = rotate(p_third, "inner", -2)
    stats = (rates, near, far)
    ds2, p_outer = block_grads("outer_grads", queries, grad_out, *stats, e2, g2, [[(1, 5)]], 1)
    outer_back = rotate(p_outer, "outer", -1)
    e4, ds2 = lax.optimization_barrier((e2, ds2))
    ds4, p_second = block_grads("second_grads", queries, grad_out, *stats, e4, g2, [[(1, 4)]], 0)
    second_back = rotate(p_second, "inner", -2)
    e1, ds4 = lax.optimization_barrier((e1, ds4))
    ds1, p_first = block_grads("first_grads", queries, grad_out, *stats, e1, g1, [[(0, 4), (1, 3)]])
    chain = (p_first.astype(F32) + third_back.astype(F32)).astype(BF16)
    chain_back = rotate(chain, "inner", -1)
    blocks = [own, first, outer, second, third]
    grad_q, p_own = own_grads(queries, grad_out, *stats, e0, g0, [ds1, ds2, ds4, ds3], blocks)
    summed = p_own + chain_back.astype(F32) + second_back.astype(F32) + outer_back.astype(F32)
    return (grad_q, summed[:, :HEAD].astype(BF16), summed[:, HEAD:].astype(BF16))


def solution(mesh):
    rows = P(("outer", "inner"), None)
    return jax.shard_map(
        body,
        mesh=mesh,
        in_specs=(rows, rows, rows, rows, P()),
        out_specs=(rows, rows, rows),
        check_vma=False,
    )
```
